512 devices in a mesh: dp: 64 (over y, z_hi, core), tensor: 8 (over z_lo, x).
Axes of the slice: x: 4, y: 8, z: 8 (z_hi: 4, z_lo: 2; z = z_hi * 2 + z_lo), core: 2. Of those that a mesh axis runs over, the one named last changes fastest.
Arguments:
- x_seq: bfloat16 [16384, 4096], P(('dp', 'tensor')), may hold values from -6 to 6
- weight: bfloat16 [4096, 2048], P(None, 'tensor'), may hold values from -0.09375 to 0.09375
- grad_out: bfloat16 [16384, 2048], P('dp', 'tensor'), may hold values from -6 to 6
- proj: bfloat16 [4096, 512], P('dp'), may hold values from -0.25 to 0.25
- moment1: float32 [512, 2048], P('dp', 'tensor'), may hold values from -6 to 6
- moment2: float32 [512, 2048], P('dp', 'tensor'), may hold values from 0.05 to 0.5
Outputs:
- values: bfloat16 [16384, 2048], P('dp', 'tensor')
- grad_in: bfloat16 [16384, 4096], P(('dp', 'tensor'))
- update: bfloat16 [4096, 2048], P(None, 'tensor')
- new_moment1: float32 [512, 2048], P('dp', 'tensor')
- new_moment2: float32 [512, 2048], P('dp', 'tensor')
The draws below stay inside these ranges and needn't reach their ends.
All inputs are finite; a program needn't handle non-finite values.
Results may differ from the reference program's by a relative error of at most 0.017.
Values may be sent and summed in bfloat16 or wider, within the bound.
No kernel may reach another device: no remote copies, remote signals or barrier semaphores. Data moves between devices by JAX's collectives and lax.ppermute only.
A program may use at most 64 MiB of HBM per device.

```python
import math
import jax
import jax.numpy as jnp
from jax import lax

D = 4096
HD = 128
RANK = 512
TOK = 256
KVH = 8
TOKENS = 16384


def block_scale(rng, dims, split, least, largest):
    def one(axis_at, parts):
        draws = jax.random.uniform(jax.random.fold_in(jax.random.fold_in(rng, 6), axis_at), (parts,), jnp.float32, least / len(split), largest / len(split))
        return jnp.repeat(jnp.exp(draws), dims[axis_at] // parts).reshape((-1,) + (1,) * (len(dims) - axis_at - 1))

    level = one(*split[0])
    for cut in split[1:]:
        level = level * one(*cut)
    return level


def bell_draw(rng, shape, scale, reach, split=(), dtype=jnp.bfloat16):
    level = block_scale(rng, shape, split, -0.22, 0.18) if split else 1.0
    result = jax.random.normal(rng, shape, jnp.float32) * scale * level
    return jnp.minimum(jnp.maximum(result, -reach), reach).astype(dtype)


def setup_inputs(seed: int = 0) -> dict:
    arg_keys = jax.random.split(jax.random.key(seed), 7)
    x_seq = bell_draw(arg_keys[0], (TOKENS, D), 1.0, 6.0, ((0, 512),))
    weight = bell_draw(arg_keys[1], (D, 2 * KVH * HD), D ** -0.5, 0.09375, ((1, 8),))
    grad_out = bell_draw(arg_keys[2], (TOKENS, 2 * KVH * HD), 1.0, 6.0, ((0, 64), (1, 8)))
    proj = bell_draw(arg_keys[3], (D, RANK), RANK ** -0.5, 0.25, ((0, 64),))
    moment1 = bell_draw(arg_keys[4], (RANK, 2 * KVH * HD), 1.0, 6.0, ((0, 64), (1, 8)), jnp.float32)
    moment2 = jnp.clip(jnp.exp(math.log(0.5) - 2.3025851 * jax.random.uniform(arg_keys[5], (RANK, 2 * KVH * HD), jnp.float32) ** block_scale(arg_keys[5], (RANK, 2 * KVH * HD), ((0, 64), (1, 8)), -0.2, 0.2)), 0.05, 0.5)
    return {"x_seq": x_seq, "weight": weight, "grad_out": grad_out, "proj": proj, "moment1": moment1, "moment2": moment2}


def reference(x_seq, weight, grad_out, proj, moment1, moment2):
    values = jnp.dot(x_seq, weight, preferred_element_type=jnp.float32).astype(jnp.bfloat16)
    summed = jnp.zeros((x_seq.shape[0], x_seq.shape[1]), jnp.float32)
    for head in range(KVH):
        head_grad = grad_out[:, head * 2 * HD:(head + 1) * 2 * HD]
        head_weight = weight[:, head * 2 * HD:(head + 1) * 2 * HD]
        partial_term = lax.dot_general(head_grad, head_weight, (((1,), (1,)), ((), ())), preferred_element_type=jnp.float32)
        summed = summed + partial_term.astype(jnp.bfloat16).astype(jnp.float32)
    grad_in = summed.astype(jnp.bfloat16)
    projected = jnp.dot(x_seq, proj, preferred_element_type=jnp.float32)
    coeff = lax.dot_general(projected, grad_out.astype(jnp.float32), (((0,), (0,)), ((), ())), precision=lax.Precision.HIGHEST)
    coeff = coeff / jnp.sqrt(jnp.float32(TOK))
    basis = proj.astype(jnp.float32)
    new_moment1 = 0.9 * moment1 + 0.1 * coeff
    new_moment2 = 0.999 * moment2 + 0.001 * coeff * coeff
    step_dir = new_moment1 / (1.0 - 0.9 ** 10) / (jnp.sqrt(new_moment2 / (1.0 - 0.999 ** 10)) + 1e-08)
    update = jnp.dot(basis, step_dir, precision=lax.Precision.HIGHEST).astype(jnp.bfloat16)
    return (values, grad_in, update, new_moment1, new_moment2)
```

```python
import math

import jax
import jax.numpy as jnp
from jax import lax
from jax.sharding import Mesh
from jax.sharding import PartitionSpec as P

AXES = ("y", "zh", "c", "zl", "x")
DP = ("y", "zh", "c")
RING = ("y", "zh")
TENSOR = ("zl", "x")
SWAP = [(0, 1), (1, 0)]


def copies_to(value, axes, count):
    copies = jnp.broadcast_to(value[None], (count, *value.shape))
    return lax.all_to_all(copies, axes, 0, 0, tiled=True)


def split(value):
    high = value.astype(jnp.bfloat16)
    return high, (value - high.astype(jnp.float32)).astype(jnp.bfloat16)


def per_device(x_seq, weight, grad_out, proj, moment1, moment2):
    first = lax.axis_index("c") == 0
    tokens, heads = grad_out.shape
    rows, rank = proj.shape
    count = 32

    def own_other(a, b):
        return jnp.where(first, a, b), jnp.where(first, b, a)

    proj_z = copies_to(proj, "zh", 4)
    x_seq, proj_z = lax.optimization_barrier((x_seq, proj_z))
    proj_own = lax.all_gather(proj_z.reshape(4 * rows, rank), "y", axis=0, tiled=True)

    x_split = x_seq.reshape(x_seq.shape[0], count, 2, rows)
    x_ordered = jnp.concatenate(own_other(x_split[:, :, 0], x_split[:, :, 1]), axis=1)
    full_x = copies_to(x_ordered.reshape(x_seq.shape), TENSOR, 8).reshape(tokens, -1)
    w_split = weight.reshape(count, 2, rows, heads)
    w_ordered = jnp.concatenate(own_other(w_split[:, 0], w_split[:, 1]), axis=0).reshape(weight.shape)
    values = jnp.dot(full_x, w_ordered, preferred_element_type=jnp.float32).astype(jnp.bfloat16)

    proj_other = lax.ppermute(proj_own, "c", SWAP)
    half = count * rows
    projected = jnp.dot(full_x[:, :half], proj_own, preferred_element_type=jnp.float32)
    projected += jnp.dot(full_x[:, half:], proj_other, preferred_element_type=jnp.float32)

    dims = (((0,), (0,)), ((), ()))
    local = sum(
        lax.dot_general(part, grad_out, dims, preferred_element_type=jnp.float32) for part in split(projected)
    )
    local = (local * (1.0 / math.sqrt(tokens))).reshape(count, 2, rank // 64, heads)
    mine, theirs = own_other(local[:, 0], local[:, 1])
    chip = mine + lax.ppermute(theirs, "c", SWAP)
    coeff = jnp.sum(lax.all_to_all(chip, RING, 0, 0, tiled=True), axis=0)

    new_moment1 = 0.9 * moment1 + 0.1 * coeff
    new_moment2 = 0.999 * moment2 + 0.001 * coeff * coeff
    step_dir = new_moment1 / (1.0 - 0.9**10) / (jnp.sqrt(new_moment2 / (1.0 - 0.999**10)) + 1e-08)

    step_own = copies_to(step_dir, RING, count)
    step = jnp.stack(own_other(step_own, lax.ppermute(step_own, "c", SWAP)), axis=1).reshape(rank, heads)
    steps = split(step)

    def update_rows(basis):
        return sum(jnp.dot(basis, part, preferred_element_type=jnp.float32) for part in steps).astype(jnp.bfloat16)

    pair = own_other(update_rows(proj_own), update_rows(proj_other))
    update = jnp.stack([u.reshape(count, rows, heads) for u in pair], axis=1).reshape(weight.shape)

    grad_out, _ = lax.optimization_barrier((grad_out, proj_other))
    grad_in = lax.psum_scatter(
        lax.dot_general(grad_out, weight, (((1,), (1,)), ((), ())), preferred_element_type=jnp.float32).astype(
            jnp.bfloat16
        ),
        TENSOR,
        scatter_dimension=0,
        tiled=True,
    )
    return (values, grad_in, update, new_moment1, new_moment2)


def solution(mesh):
    fine = Mesh(mesh.devices.reshape(8, 4, 2, 2, 4), AXES)
    placed = (P(AXES, None), P(None, TENSOR), P(DP, TENSOR), P(DP, None), P(DP, TENSOR), P(DP, TENSOR))
    return jax.shard_map(
        per_device,
        mesh=fine,
        in_specs=placed,
        out_specs=(P(DP, TENSOR), P(AXES, None), P(None, TENSOR), P(DP, TENSOR), P(DP, TENSOR)),
        check_vma=False,
    )
```

```python
import math

import jax
import jax.numpy as jnp
from jax import lax
from jax.experimental import pallas as pl
from jax.experimental.pallas import tpu as pltpu
from jax.sharding import Mesh
from jax.sharding import PartitionSpec as P

AXES = ("y", "zh", "c", "zl", "x")
DP = ("y", "zh", "c")
RING = ("y", "zh")
TENSOR = ("zl", "x")
SWAP = [(0, 1), (1, 0)]
bf16, f32 = jnp.bfloat16, jnp.float32


def copies_to(value, axes, count):
    copies = jnp.broadcast_to(value[None], (count, *value.shape))
    return lax.all_to_all(copies, axes, 0, 0, tiled=True)


def update_rows(cores, basis_own, basis_other, step, rows):
    parts, half, width = basis_own.shape
    heads = step.shape[1]
    blocks = 4

    def kernel(core_ref, own_ref, other_ref, step_ref, out_ref):
        for ref, place in ((own_ref, core_ref[0]), (other_ref, core_ref[1])):
            for i in range(half // (blocks * rows)):
                lines = slice(i * blocks * rows, (i + 1) * blocks * rows)
                line = jnp.concatenate([ref[k, lines, :] for k in range(parts)], axis=1)
                block = jnp.dot(line, step_ref[...], preferred_element_type=f32).astype(bf16)
                out_ref[i * blocks : (i + 1) * blocks, pl.ds(place, 1)] = block.reshape(blocks, 1, rows, heads)

    vmem = pl.BlockSpec(memory_space=pltpu.VMEM)
    out = pl.pallas_call(
        kernel,
        out_shape=jax.ShapeDtypeStruct((half // rows, 2, rows, heads), bf16),
        in_specs=[pl.BlockSpec(memory_space=pltpu.SMEM), vmem, vmem, vmem],
        out_specs=vmem,
        compiler_params=pltpu.CompilerParams(vmem_limit_bytes=24 * 2**20),
        cost_estimate=pl.CostEstimate(
            flops=4 * half * parts * width * heads,
            bytes_accessed=4 * half * (parts * width + heads),
            transcendentals=0,
        ),
    )(cores, basis_own, basis_other, step)
    return out.reshape(2 * half, heads)


def per_device(x_seq, weight, grad_out, proj, moment1, moment2):
    core = lax.axis_index("c")
    first = core == 0
    tokens, heads = grad_out.shape
    rows, rank = proj.shape
    features = weight.shape[0]
    own_tokens = x_seq.shape[0]
    count = 32
    half = count * rows
    dims = (((0,), (0,)), ((), ()))

    def ordered(own, other):
        return [jnp.where(first, own, other), jnp.where(first, other, own)]

    def swap(value):
        return lax.ppermute(value, "c", SWAP)

    proj_z = copies_to(proj, "zh", 4)
    x_seq, grad_out, moment1, proj_z = lax.optimization_barrier((x_seq, grad_out, moment1, proj_z))
    proj_own = lax.all_gather(proj_z.reshape(4 * rows, rank), "y", axis=0, tiled=True)

    x_split = x_seq.reshape(own_tokens, count, 2, rows)
    x_own, x_other = (v.reshape(own_tokens, half) for v in ordered(x_split[:, :, 0], x_split[:, :, 1]))
    both_x = copies_to(jnp.stack([x_own, swap(x_other)]), TENSOR, 8).reshape(2 * tokens, half)

    terms = lax.dot_general(grad_out, weight, (((1,), (1,)), ((), ())), preferred_element_type=f32).astype(bf16)
    grads = [g.reshape(8, own_tokens, heads) for g in (grad_out, swap(grad_out))]
    both_grads = jnp.stack(grads, axis=1).reshape(2 * tokens, heads)
    moments = jnp.stack([moment1, moment2])
    moments = jnp.stack(ordered(moments, swap(moments)), axis=1).reshape(2, 2 * moment1.shape[0], heads)
    proj_own, terms, both_grads, moments = lax.optimization_barrier((proj_own, terms, both_grads, moments))
    grad_in = lax.psum_scatter(terms, TENSOR, scatter_dimension=0, tiled=True)

    projected = jnp.dot(both_x, proj_own, preferred_element_type=f32).astype(bf16)
    projected = lax.optimization_barrier(projected)
    local = lax.dot_general(projected, both_grads, dims, preferred_element_type=f32)
    local = (local * (1.0 / math.sqrt(tokens))).astype(bf16).reshape(count, -1, heads)
    chip = jnp.sum(lax.all_to_all(local, RING, 0, 0, tiled=True).astype(f32), axis=0)
    coeff = chip + swap(chip)
    both1 = 0.9 * moments[0] + 0.1 * coeff
    both2 = 0.999 * moments[1] + 0.001 * coeff * coeff
    step_dir = both1 / (1.0 - 0.9**10) / (jnp.sqrt(both2 / (1.0 - 0.999**10)) + 1e-08)
    new_moment1, new_moment2 = (jnp.where(first, m[:8], m[8:]) for m in (both1, both2))

    proj_other = swap(proj_own)
    w_split = weight.reshape(count, 2, rows, heads)
    w_own = jnp.where(first, w_split[:, 0], w_split[:, 1]).reshape(half, heads)
    parts = jnp.dot(both_x, w_own, preferred_element_type=f32).reshape(8, 2, own_tokens, heads)
    values = (parts[:, 0] + swap(parts[:, 1])).astype(bf16).reshape(tokens, heads)

    step = copies_to(step_dir.astype(bf16), RING, count).reshape(rank, heads)
    update = update_rows(jnp.stack([core, 1 - core]), proj_own[None], proj_other[None], step, rows)
    return (values, grad_in, update, new_moment1, new_moment2)


def solution(mesh):
    fine = Mesh(mesh.devices.reshape(8, 4, 2, 2, 4), AXES)
    placed = (P(AXES, None), P(None, TENSOR), P(DP, TENSOR), P(DP, None), P(DP, TENSOR), P(DP, TENSOR))
    return jax.shard_map(
        per_device,
        mesh=fine,
        in_specs=placed,
        out_specs=(P(DP, TENSOR), P(AXES, None), P(None, TENSOR), P(DP, TENSOR), P(DP, TENSOR)),
        check_vma=False,
    )
```

```python
import math

import jax
import jax.numpy as jnp
from jax import lax
from jax.experimental import pallas as pl
from jax.experimental.pallas import tpu as pltpu
from jax.sharding import Mesh
from jax.sharding import PartitionSpec as P

AXES = ("y", "zh", "c", "zl", "x")
DP = ("y", "zh", "c")
RING = ("y", "zh")
TENSOR = ("zl", "x")
SWAP = [(0, 1), (1, 0)]
bf16, f32 = jnp.bfloat16, jnp.float32


def copies_to(value, axes, count):
    copies = jnp.broadcast_to(value[None], (count, *value.shape))
    return lax.all_to_all(copies, axes, 0, 0, tiled=True)


def update_rows(cores, basis_own, basis_other, step, rows):
    parts, half, width = basis_own.shape
    heads = step.shape[1]
    blocks = 16

    def kernel(core_ref, own_ref, other_ref, step_ref, out_ref):
        for ref, place in ((own_ref, core_ref[0]), (other_ref, core_ref[1])):
            for i in range(half // (blocks * rows)):
                lines = slice(i * blocks * rows, (i + 1) * blocks * rows)
                line = jnp.concatenate([ref[k, lines, :] for k in range(parts)], axis=1)
                block = jnp.dot(line, step_ref[...], preferred_element_type=f32).astype(bf16)
                out_ref[i * blocks : (i + 1) * blocks, pl.ds(place, 1)] = block.reshape(blocks, 1, rows, heads)

    vmem = pl.BlockSpec(memory_space=pltpu.VMEM)
    out = pl.pallas_call(
        kernel,
        out_shape=jax.ShapeDtypeStruct((half // rows, 2, rows, heads), bf16),
        in_specs=[pl.BlockSpec(memory_space=pltpu.SMEM), vmem, vmem, vmem],
        out_specs=vmem,
        compiler_params=pltpu.CompilerParams(vmem_limit_bytes=24 * 2**20),
        cost_estimate=pl.CostEstimate(
            flops=4 * half * parts * width * heads,
            bytes_accessed=4 * half * (parts * width + heads),
            transcendentals=0,
        ),
    )(cores, basis_own, basis_other, step)
    return out.reshape(2 * half, heads)


def per_device(x_seq, weight, grad_out, proj, moment1, moment2):
    core = lax.axis_index("c")
    first = core == 0
    tokens, heads = grad_out.shape
    rows, rank = proj.shape
    features = weight.shape[0]
    own_tokens = x_seq.shape[0]
    count = 32
    half = count * rows
    dims = (((0,), (0,)), ((), ()))

    def ordered(own, other):
        return [jnp.where(first, own, other), jnp.where(first, other, own)]

    def swap(value):
        return lax.ppermute(value, "c", SWAP)

    proj_z = copies_to(proj, "zh", 4)
    x_seq, grad_out, moment1, proj_z = lax.optimization_barrier((x_seq, grad_out, moment1, proj_z))
    proj_own = lax.all_gather(proj_z.reshape(4 * rows, rank), "y", axis=0, tiled=True)

    x_split = x_seq.reshape(own_tokens, count, 2, rows)
    x_own, x_other = (v.reshape(own_tokens, half) for v in ordered(x_split[:, :, 0], x_split[:, :, 1]))
    both_x = copies_to(jnp.stack([x_own, swap(x_other)]), TENSOR, 8).reshape(2 * tokens, half)

    by_x = grad_out.reshape(2, 4, own_tokens, heads).transpose(1, 0, 2, 3).reshape(tokens, heads)
    terms = lax.dot_general(by_x, weight, (((1,), (1,)), ((), ())), preferred_element_type=f32).astype(bf16)
    grads = [g.reshape(8, own_tokens, heads) for g in (grad_out, swap(grad_out))]
    both_grads = jnp.stack(grads, axis=1).reshape(2 * tokens, heads)
    moments = jnp.stack([moment1, moment2])
    moments = jnp.stack(ordered(moments, swap(moments)), axis=1).reshape(2, 2 * moment1.shape[0], heads)
    w_split = weight.reshape(count, 2, rows, heads)
    w_own = jnp.where(first, w_split[:, 0], w_split[:, 1]).reshape(half, heads)
    proj_own, terms, both_grads, moments, w_own = lax.optimization_barrier(
        (proj_own, terms, both_grads, moments, w_own)
    )
    met = lax.psum_scatter(terms, "x", scatter_dimension=0, tiled=True)

    projected = jnp.dot(both_x, proj_own, preferred_element_type=f32).astype(bf16)
    projected, proj_own = lax.optimization_barrier((projected, proj_own))
    local = lax.dot_general(projected, both_grads, dims, preferred_element_type=f32)
    local = (local * (1.0 / math.sqrt(tokens))).astype(bf16).reshape(count, -1, heads)
    chip = jnp.sum(lax.all_to_all(local, RING, 0, 0, tiled=True).astype(f32), axis=0)
    parts = jnp.dot(both_x, w_own, preferred_element_type=f32).reshape(8, 2, own_tokens, heads)
    chip, theirs = lax.optimization_barrier((chip, swap(parts[:, 1])))
    values = (parts[:, 0] + theirs).astype(bf16).reshape(tokens, heads)

    coeff = chip + swap(chip)
    both1 = 0.9 * moments[0] + 0.1 * coeff
    both2 = 0.999 * moments[1] + 0.001 * coeff * coeff
    step_dir = both1 / (1.0 - 0.9**10) / (jnp.sqrt(both2 / (1.0 - 0.999**10)) + 1e-08)
    new_moment1, new_moment2 = (jnp.where(first, m[:8], m[8:]) for m in (both1, both2))
    proj_other = swap(proj_own)
    step = copies_to(step_dir.astype(bf16), RING, count).reshape(rank, heads)

    new_moment1, met = lax.optimization_barrier((new_moment1, met))
    met = met.reshape(2, own_tokens, features)
    zl = lax.axis_index("zl")
    far = lax.ppermute(lax.dynamic_index_in_dim(met, 1 - zl, axis=0, keepdims=False), "zl", SWAP)
    near = lax.dynamic_index_in_dim(met, zl, axis=0, keepdims=False)
    grad_in = (near.astype(f32) + far.astype(f32)).astype(bf16)
    update = update_rows(jnp.stack([core, 1 - core]), proj_own[None], proj_other[None], step, rows)
    return (values, grad_in, update, new_moment1, new_moment2)


def solution(mesh):
    fine = Mesh(mesh.devices.reshape(8, 4, 2, 2, 4), AXES)
    placed = (P(AXES, None), P(None, TENSOR), P(DP, TENSOR), P(DP, None), P(DP, TENSOR), P(DP, TENSOR))
    return jax.shard_map(
        per_device,
        mesh=fine,
        in_specs=placed,
        out_specs=(P(DP, TENSOR), P(AXES, None), P(None, TENSOR), P(DP, TENSOR), P(DP, TENSOR)),
        check_vma=False,
    )
```

```python
import math

import jax
import jax.numpy as jnp
from jax import lax
from jax.experimental import pallas as pl
from jax.experimental.pallas import tpu as pltpu
from jax.sharding import Mesh
from jax.sharding import PartitionSpec as P

AXES = ("y", "zh", "c", "zl", "x")
DP = ("y", "zh", "c")
RING = ("y", "zh")
TENSOR = ("zl", "x")
SWAP = [(0, 1), (1, 0)]
bf16, f32 = jnp.bfloat16, jnp.float32


def copies_to(value, axes, count):
    copies = jnp.broadcast_to(value[None], (count, *value.shape))
    return lax.all_to_all(copies, axes, 0, 0, tiled=True)


def update_rows(cores, basis_own, basis_other, step, rows):
    parts, half, width = basis_own.shape
    heads = step.shape[1]
    blocks = 16

    def kernel(core_ref, own_ref, other_ref, step_ref, out_ref):
        for ref, place in ((own_ref, core_ref[0]), (other_ref, core_ref[1])):
            for i in range(half // (blocks * rows)):
                lines = slice(i * blocks * rows, (i + 1) * blocks * rows)
                line = jnp.concatenate([ref[k, lines, :] for k in range(parts)], axis=1)
                block = jnp.dot(line, step_ref[...], preferred_element_type=f32).astype(bf16)
                out_ref[i * blocks : (i + 1) * blocks, pl.ds(place, 1)] = block.reshape(blocks, 1, rows, heads)

    vmem = pl.BlockSpec(memory_space=pltpu.VMEM)
    out = pl.pallas_call(
        kernel,
        out_shape=jax.ShapeDtypeStruct((half // rows, 2, rows, heads), bf16),
        in_specs=[pl.BlockSpec(memory_space=pltpu.SMEM), vmem, vmem, vmem],
        out_specs=vmem,
        compiler_params=pltpu.CompilerParams(vmem_limit_bytes=24 * 2**20),
        cost_estimate=pl.CostEstimate(
            flops=4 * half * parts * width * heads,
            bytes_accessed=4 * half * (parts * width + heads),
            transcendentals=0,
        ),
    )(cores, basis_own, basis_other, step)
    return out.reshape(2 * half, heads)


def per_device(x_seq, weight, grad_out, proj, moment1, moment2):
    core = lax.axis_index("c")
    first = core == 0
    tokens, heads = grad_out.shape
    rows, rank = proj.shape
    features = weight.shape[0]
    own_tokens = x_seq.shape[0]
    count = 32
    half = count * rows
    dims = (((0,), (0,)), ((), ()))

    def ordered(own, other):
        return [jnp.where(first, own, other), jnp.where(first, other, own)]

    def swap(value):
        return lax.ppermute(value, "c", SWAP)

    proj_z = copies_to(proj, "zh", 4)
    x_seq, grad_out, moment1, proj_z = lax.optimization_barrier((x_seq, grad_out, moment1, proj_z))
    proj_own = lax.all_gather(proj_z.reshape(4 * rows, rank), "y", axis=0, tiled=True)

    x_split = x_seq.reshape(own_tokens, count, 2, rows)
    x_own, x_other = (v.reshape(own_tokens, half) for v in ordered(x_split[:, :, 0], x_split[:, :, 1]))
    both_x = copies_to(jnp.stack([x_own, swap(x_other)]), TENSOR, 8).reshape(2 * tokens, half)

    by_x = grad_out.reshape(2, 4, own_tokens, heads).transpose(1, 0, 2, 3).reshape(tokens, heads)
    terms = lax.dot_general(by_x, weight, (((1,), (1,)), ((), ())), preferred_element_type=f32).astype(bf16)
    grads = [g.reshape(8, own_tokens, heads) for g in (grad_out, swap(grad_out))]
    both_grads = jnp.stack(grads, axis=1).reshape(2 * tokens, heads)
    w_split = weight.reshape(count, 2, rows, heads)
    w_own = jnp.where(first, w_split[:, 0], w_split[:, 1]).reshape(half, heads)
    proj_own, terms, both_grads, w_own = lax.optimization_barrier((proj_own, terms, both_grads, w_own))
    met = lax.psum_scatter(terms, "x", scatter_dimension=0, tiled=True)

    projected = jnp.dot(both_x, proj_own, preferred_element_type=f32).astype(bf16)
    projected = lax.optimization_barrier(projected)
    local = lax.dot_general(projected, both_grads, dims, preferred_element_type=f32)
    local = (local * (1.0 / math.sqrt(tokens))).astype(bf16).reshape(2 * count, -1, heads)
    coeff = jnp.sum(lax.all_to_all(local, DP, 0, 0, tiled=True).astype(f32), axis=0)

    parts = jnp.dot(both_x, w_own, preferred_element_type=f32).reshape(8, 2, own_tokens, heads)
    coeff, theirs, proj_own = lax.optimization_barrier((coeff, swap(parts[:, 1]), proj_own))
    values = (parts[:, 0] + theirs).astype(bf16).reshape(tokens, heads)

    new_moment1 = 0.9 * moment1 + 0.1 * coeff
    new_moment2 = 0.999 * moment2 + 0.001 * coeff * coeff
    step_dir = new_moment1 / (1.0 - 0.9**10) / (jnp.sqrt(new_moment2 / (1.0 - 0.999**10)) + 1e-08)
    proj_other = swap(proj_own)
    step = copies_to(step_dir.astype(bf16), DP, 2 * count).reshape(rank, heads)

    new_moment1, met = lax.optimization_barrier((new_moment1, met))
    met = met.reshape(2, own_tokens, features)
    zl = lax.axis_index("zl")
    far = lax.ppermute(lax.dynamic_index_in_dim(met, 1 - zl, axis=0, keepdims=False), "zl", SWAP)
    near = lax.dynamic_index_in_dim(met, zl, axis=0, keepdims=False)
    grad_in = (near.astype(f32) + far.astype(f32)).astype(bf16)
    update = update_rows(jnp.stack([core, 1 - core]), proj_own[None], proj_other[None], step, rows)
    return (values, grad_in, update, new_moment1, new_moment2)


def solution(mesh):
    fine = Mesh(mesh.devices.reshape(8, 4, 2, 2, 4), AXES)
    placed = (P(AXES, None), P(None, TENSOR), P(DP, TENSOR), P(DP, None), P(DP, TENSOR), P(DP, TENSOR))
    return jax.shard_map(
        per_device,
        mesh=fine,
        in_specs=placed,
        out_specs=(P(DP, TENSOR), P(AXES, None), P(None, TENSOR), P(DP, TENSOR), P(DP, TENSOR)),
        check_vma=False,
    )
```

```python
import math

import jax
import jax.numpy as jnp
from jax import lax
from jax.experimental import pallas as pl
from jax.experimental.pallas import tpu as pltpu
from jax.sharding import Mesh
from jax.sharding import PartitionSpec as P

AXES = ("y", "zh", "c", "zl", "x")
DP = ("y", "zh", "c")
RING = ("y", "zh")
TENSOR = ("zl", "x")
SWAP = [(0, 1), (1, 0)]
bf16, f32 = jnp.bfloat16, jnp.float32


def copies_to(value, axes, count):
    copies = jnp.broadcast_to(value[None], (count, *value.shape))
    return lax.all_to_all(copies, axes, 0, 0, tiled=True)


def update_rows(cores, basis_own, basis_other, step, rows):
    parts, half, width = basis_own.shape
    heads = step.shape[1]
    blocks = 16

    def kernel(core_ref, own_ref, other_ref, step_ref, out_ref):
        for ref, place in ((own_ref, core_ref[0]), (other_ref, core_ref[1])):
            for i in range(half // (blocks * rows)):
                lines = slice(i * blocks * rows, (i + 1) * blocks * rows)
                line = jnp.concatenate([ref[k, lines, :] for k in range(parts)], axis=1)
                block = jnp.dot(line, step_ref[...], preferred_element_type=f32).astype(bf16)
                out_ref[i * blocks : (i + 1) * blocks, pl.ds(place, 1)] = block.reshape(blocks, 1, rows, heads)

    vmem = pl.BlockSpec(memory_space=pltpu.VMEM)
    out = pl.pallas_call(
        kernel,
        out_shape=jax.ShapeDtypeStruct((half // rows, 2, rows, heads), bf16),
        in_specs=[pl.BlockSpec(memory_space=pltpu.SMEM), vmem, vmem, vmem],
        out_specs=vmem,
        compiler_params=pltpu.CompilerParams(vmem_limit_bytes=24 * 2**20),
        cost_estimate=pl.CostEstimate(
            flops=4 * half * parts * width * heads,
            bytes_accessed=4 * half * (parts * width + heads),
            transcendentals=0,
        ),
    )(cores, basis_own, basis_other, step)
    return out.reshape(2 * half, heads)


def per_device(x_seq, weight, grad_out, proj, moment1, moment2):
    core = lax.axis_index("c")
    first = core == 0
    tokens, heads = grad_out.shape
    rows, rank = proj.shape
    features = weight.shape[0]
    own_tokens = x_seq.shape[0]
    count = 32
    half = count * rows
    dims = (((0,), (0,)), ((), ()))

    def ordered(own, other):
        return [jnp.where(first, own, other), jnp.where(first, other, own)]

    def swap(value):
        return lax.ppermute(value, "c", SWAP)

    proj_z = lax.all_gather(proj, "zh", axis=0, tiled=False)
    x_seq, grad_out, moment1, proj_z = lax.optimization_barrier((x_seq, grad_out, moment1, proj_z))
    proj_own = lax.all_gather(proj_z.reshape(4 * rows, rank), "y", axis=0, tiled=True)

    x_split = x_seq.reshape(own_tokens, count, 2, rows)
    x_own, x_other = (v.reshape(own_tokens, half) for v in ordered(x_split[:, :, 0], x_split[:, :, 1]))
    both_x = copies_to(jnp.stack([x_own, swap(x_other)]), TENSOR, 8).reshape(2 * tokens, half)

    by_x = grad_out.reshape(2, 4, own_tokens, heads).transpose(1, 0, 2, 3).reshape(tokens, heads)
    terms = lax.dot_general(by_x, weight, (((1,), (1,)), ((), ())), preferred_element_type=f32).astype(bf16)
    grads = [g.reshape(8, own_tokens, heads) for g in (grad_out, swap(grad_out))]
    both_grads = jnp.stack(grads, axis=1).reshape(2 * tokens, heads)
    moments = jnp.stack([moment1, moment2])
    moments = jnp.stack(ordered(moments, swap(moments)), axis=1).reshape(2, 2 * moment1.shape[0], heads)
    w_split = weight.reshape(count, 2, rows, heads)
    w_own = jnp.where(first, w_split[:, 0], w_split[:, 1]).reshape(half, heads)
    proj_own, terms, both_grads, moments, w_own = lax.optimization_barrier(
        (proj_own, terms, both_grads, moments, w_own)
    )
    met = lax.psum_scatter(terms, "x", scatter_dimension=0, tiled=True)

    projected = jnp.dot(both_x, proj_own, preferred_element_type=f32).astype(bf16)
    projected, proj_own = lax.optimization_barrier((projected, proj_own))
    local = lax.dot_general(projected, both_grads, dims, preferred_element_type=f32)
    local = (local * (1.0 / math.sqrt(tokens))).astype(bf16).reshape(count, -1, heads)
    chip = jnp.sum(lax.all_to_all(local, RING, 0, 0, tiled=True).astype(f32), axis=0)
    parts = jnp.dot(both_x, w_own, preferred_element_type=f32).reshape(8, 2, own_tokens, heads)
    chip, theirs = lax.optimization_barrier((chip, swap(parts[:, 1])))
    values = (parts[:, 0] + theirs).astype(bf16).reshape(tokens, heads)

    coeff = chip + swap(chip)
    both1 = 0.9 * moments[0] + 0.1 * coeff
    both2 = 0.999 * moments[1] + 0.001 * coeff * coeff
    step_dir = both1 / (1.0 - 0.9**10) / (jnp.sqrt(both2 / (1.0 - 0.999**10)) + 1e-08)
    new_moment1, new_moment2 = (jnp.where(first, m[:8], m[8:]) for m in (both1, both2))
    proj_other = swap(proj_own)
    step = copies_to(step_dir.astype(bf16), RING, count).reshape(rank, heads)

    new_moment1, met = lax.optimization_barrier((new_moment1, met))
    met = met.reshape(2, own_tokens, features)
    zl = lax.axis_index("zl")
    far = lax.ppermute(lax.dynamic_index_in_dim(met, 1 - zl, axis=0, keepdims=False), "zl", SWAP)
    near = lax.dynamic_index_in_dim(met, zl, axis=0, keepdims=False)
    grad_in = (near.astype(f32) + far.astype(f32)).astype(bf16)
    update = update_rows(jnp.stack([core, 1 - core]), proj_own[None], proj_other[None], step, rows)
    return (values, grad_in, update, new_moment1, new_moment2)


def solution(mesh):
    fine = Mesh(mesh.devices.reshape(8, 4, 2, 2, 4), AXES)
    placed = (P(AXES, None), P(None, TENSOR), P(DP, TENSOR), P(DP, None), P(DP, TENSOR), P(DP, TENSOR))
    return jax.shard_map(
        per_device,
        mesh=fine,
        in_specs=placed,
        out_specs=(P(DP, TENSOR), P(AXES, None), P(None, TENSOR), P(DP, TENSOR), P(DP, TENSOR)),
        check_vma=False,
    )
```
